128 devices in a mesh: row: 8 (over z, core), col: 16 (over y, x).
Axes of the slice: x: 4, y: 4, z: 4, core: 2. Of those that a mesh axis runs over, the one named last changes fastest.
Arguments:
- tokens: bfloat16 [2048, 8192], P('col', 'row'), may hold values from -6 to 6
- out_grad: bfloat16 [2048, 8192], P('col', 'row'), may hold values from -6 to 6
- gate_weight: bfloat16 [8192, 14336], P('row', 'col'), may hold values from -0.0625 to 0.0625
- up_weight: bfloat16 [8192, 14336], P('row', 'col'), may hold values from -0.0625 to 0.0625
- down_weight: bfloat16 [14336, 8192], P('col', 'row'), may hold values from -0.046875 to 0.046875
Outputs:
- input_grad: bfloat16 [2048, 8192], P('col', 'row')
- gate_weight_grad: bfloat16 [8192, 14336], P('row', 'col')
- up_weight_grad: bfloat16 [8192, 14336], P('row', 'col')
- down_weight_grad: bfloat16 [14336, 8192], P('col', 'row')
The draws below stay inside these ranges and needn't reach their ends.
All inputs are finite; a program needn't handle non-finite values.
Results may differ from the reference program's by a relative error of at most 0.034.
Values may be sent and summed in bfloat16 or wider, within the bound.
No kernel may reach another device: no remote copies, remote signals or barrier semaphores. Data moves between devices by JAX's collectives and lax.ppermute only.
A program may use at most 128 MiB of HBM per device.

```python
import jax
import jax.numpy as jnp
from jax import lax

D = 8192
FF = 14336
TOKENS = 2048
N_ROW = 8


def levels(stream_key, dims, shards, low, top_value):
    def one(dim, parts):
        draws = jax.random.uniform(jax.random.fold_in(jax.random.fold_in(stream_key, 6), dim), (parts,), jnp.float32, low / len(shards), top_value / len(shards))
        return jnp.repeat(jnp.exp(draws), dims[dim] // parts).reshape((-1,) + (1,) * (len(dims) - dim - 1))

    loudness = one(*shards[0])
    for cut in shards[1:]:
        loudness = loudness * one(*cut)
    return loudness


def bell_draw(key, shape, width, limit, pieces=(), kind=jnp.bfloat16):
    loudness = levels(key, shape, pieces, -0.22, 0.18) if pieces else 1.0
    values = jax.random.normal(key, shape, jnp.float32) * width * loudness
    return jnp.minimum(jnp.maximum(values, -limit), limit).astype(kind)


def setup_inputs(seed: int = 0) -> dict:
    seeds = jax.random.split(jax.random.key(seed), 6)
    tokens = bell_draw(seeds[0], (TOKENS, D), 1.0, 6.0, ((0, 16), (1, 8)))
    out_grad = bell_draw(seeds[1], (TOKENS, D), 0.5, 6.0, ((0, 16), (1, 8)))
    gate_weight = bell_draw(seeds[2], (D, FF), D ** -0.5, 0.0625, ((0, 8), (1, 16)))
    up_weight = bell_draw(seeds[3], (D, FF), D ** -0.5, 0.0625, ((0, 8), (1, 16)))
    down_weight = bell_draw(seeds[4], (FF, D), FF ** -0.5, 0.046875, ((0, 16), (1, 8)))
    return dict(tokens=tokens, out_grad=out_grad, gate_weight=gate_weight, up_weight=up_weight, down_weight=down_weight)


def contract_last(left, right):
    return lax.dot_general(left, right, (((1,), (1,)), ((), ())), preferred_element_type=jnp.float32)


def contract_first(left, right):
    return lax.dot_general(left, right, (((0,), (0,)), ((), ())), preferred_element_type=jnp.float32)


def activate(gate_sum, up_sum, back_sum):
    sigma = jax.nn.sigmoid(gate_sum)
    hidden = (gate_sum * sigma * up_sum).astype(jnp.bfloat16)
    up_grad = (back_sum * gate_sum * sigma).astype(jnp.bfloat16)
    gate_grad = (back_sum * up_sum * sigma * (1.0 + gate_sum * (1.0 - sigma))).astype(jnp.bfloat16)
    return hidden, gate_grad, up_grad


def reference(tokens, out_grad, gate_weight, up_weight, down_weight):
    block_width = D // N_ROW

    def add_block(carry, index):
        first = (index * block_width).astype(jnp.int32)
        token_block = lax.dynamic_slice_in_dim(tokens, first, block_width, 1)
        grad_block = lax.dynamic_slice_in_dim(out_grad, first, block_width, 1)
        gate_block = lax.dynamic_slice_in_dim(gate_weight, first, block_width, 0)
        up_block = lax.dynamic_slice_in_dim(up_weight, first, block_width, 0)
        down_block = lax.dynamic_slice_in_dim(down_weight, first, block_width, 1)
        terms = (jnp.dot(token_block, gate_block, preferred_element_type=jnp.float32),
                 jnp.dot(token_block, up_block, preferred_element_type=jnp.float32),
                 contract_last(grad_block, down_block))
        rounded = lax.optimization_barrier(tuple(term.astype(jnp.bfloat16) for term in terms))
        return tuple(acc + part.astype(jnp.float32) for acc, part in zip(carry, rounded)), None

    zeros = jnp.zeros((TOKENS, FF), jnp.float32)
    sums, _ = lax.scan(add_block, (zeros, zeros, zeros), jnp.arange(N_ROW, dtype=jnp.int32))
    hidden, gate_grad, up_grad = activate(sums[0], sums[1], sums[2])
    down_weight_grad = contract_first(hidden, out_grad).astype(jnp.bfloat16)
    gate_weight_grad = contract_first(tokens, gate_grad).astype(jnp.bfloat16)
    up_weight_grad = contract_first(tokens, up_grad).astype(jnp.bfloat16)
    input_grad = (contract_last(gate_grad, gate_weight) + contract_last(up_grad, up_weight)).astype(jnp.bfloat16)
    return input_grad, gate_weight_grad, up_weight_grad, down_weight_grad
```

```python
import jax
import jax.numpy as jnp
import numpy as np
from jax import lax
from jax.experimental import pallas as pl
from jax.experimental.pallas import tpu as pltpu
from jax.sharding import PartitionSpec as P

AXES = ("row", "col")
NZ, NC, NY, NX = 4, 2, 4, 4
BF, F32 = jnp.bfloat16, jnp.float32


def dev(z, c, y, x):
    return ((z % NZ) * NC + c) * (NY * NX) + (y % NY) * NX + x % NX


def grid_pairs(target):
    pairs = []
    for z in range(NZ):
        for c in range(NC):
            for y in range(NY):
                for x in range(NX):
                    pairs.append((dev(z, c, y, x), target(z, c, y, x)))
    return pairs


def along_first(step):
    return grid_pairs(lambda z, c, y, x: dev(z, c, y, x + step) if c == 0 else dev(z, c, y + step, x))


def along_second(step):
    return grid_pairs(lambda z, c, y, x: dev(z, c, y + step, x) if c == 0 else dev(z, c, y, x + step))


def along_z(step):
    return grid_pairs(lambda z, c, y, x: dev(z + step if c == 0 else z - step, c, y, x))


def to_partner():
    return grid_pairs(lambda z, c, y, x: dev(z, 1 - c, y, x))


def permute(value, pairs):
    return lax.ppermute(value, AXES, pairs)


def dot(left, right, dims):
    return lax.dot_general(left, right, (dims, ((), ())), preferred_element_type=F32)


def order_of(core, z):
    places = []
    for half in range(2):
        owner = (core + half) % 2
        sign = 1 - 2 * owner
        for k in range(NZ):
            places.append(owner * NZ + (z + sign * k + NZ) % NZ)
    return jnp.stack(places).astype(jnp.int32)


def reorder(order, tokens, out_grad):
    def body(order_ref, t_ref, g_ref, to_ref, go_ref):
        to_ref[...] = t_ref[...]
        go_ref[...] = g_ref[...]

    rows, width = tokens.shape
    piece = rows // 8
    spec_in = pl.BlockSpec((1, piece, width), lambda i, order_ref: (order_ref[i], 0, 0))
    spec_out = pl.BlockSpec((1, piece, width), lambda i, order_ref: (i, 0, 0))
    shape = jax.ShapeDtypeStruct((8, piece, width), BF)
    return pl.pallas_call(
        body,
        grid_spec=pltpu.PrefetchScalarGridSpec(
            num_scalar_prefetch=1, grid=(8,), in_specs=[spec_in] * 2, out_specs=[spec_out] * 2
        ),
        out_shape=[shape, shape],
    )(order, tokens.reshape(8, piece, width), out_grad.reshape(8, piece, width))


def gather(piece):
    first = jnp.stack([piece] + [permute(piece, along_first(-s)) for s in (1, 2, 3)])
    second = jnp.stack([first] + [permute(first, along_second(-s)) for s in (1, 2, 3)])
    _, _, _, rows, width = second.shape
    return second.reshape(4, 4, 2, 4, rows, width).transpose(2, 3, 0, 1, 4, 5)


def scatter_sum(value):
    got = [permute(value[:, :, s], along_second(s)) for s in (1, 2, 3)]
    part = sum((g.astype(F32) for g in got), value[:, :, 0].astype(F32)).astype(BF)
    got = [permute(part[:, :, s], along_first(s)) for s in (1, 2, 3)]
    return sum((g.astype(F32) for g in got), part[:, :, 0].astype(F32))


def swap_blocks(value):
    return jnp.swapaxes(value, 1, 2)


def term(rows, weight, dims):
    lead = rows.shape[:-1]
    out = dot(rows.reshape(-1, rows.shape[-1]), weight, dims).astype(BF)
    return out.reshape(*lead, out.shape[-1])


def reduce_z(mine, theirs):
    def both(k):
        return mine[k].astype(F32) + jnp.swapaxes(theirs[k], 0, 1).astype(F32)

    moving = both(3).astype(BF)
    for k in (2, 1):
        moving = (permute(moving, along_z(1)).astype(F32) + both(k)).astype(BF)
    return permute(moving, along_z(1)).astype(F32) + both(0)


def gather_z(piece):
    pieces = {0: piece}
    moving = piece
    for k in (3, 2, 1):
        moving = permute(moving, along_z(1))
        pieces[k] = moving
    mine = jnp.stack([pieces[k] for k in range(NZ)])
    theirs = swap_blocks(permute(mine, to_partner()))
    return jnp.stack([mine, theirs])


def on_device(tokens, out_grad, gate_weight, up_weight, down_weight):
    row = lax.axis_index("row")
    z, core = row // NC, row % NC
    order = order_of(core, z)
    rows, width = tokens.shape
    token_piece, grad_piece = reorder(order, tokens, out_grad)

    token_all = gather(token_piece)
    grad_all = gather(grad_piece)

    sums = []
    for left, weight, dims in (
        (token_all, gate_weight, ((1,), (0,))),
        (token_all, up_weight, ((1,), (0,))),
        (grad_all, down_weight, ((1,), (1,))),
    ):
        theirs = permute(term(left[1], weight, dims), to_partner())
        sums.append(reduce_z(term(left[0], weight, dims), theirs))
    gate_sum, up_sum, back_sum = sums
    sigma = jax.nn.sigmoid(gate_sum)
    hidden = (gate_sum * sigma * up_sum).astype(BF)
    up_grad = (back_sum * gate_sum * sigma).astype(BF)
    gate_grad = (back_sum * up_sum * sigma * (1.0 + gate_sum * (1.0 - sigma))).astype(BF)

    gate_grad_all = gather_z(gate_grad)
    up_grad_all = gather_z(up_grad)
    hidden_all = gather_z(hidden)

    def flat(value):
        return value.reshape(-1, value.shape[-1])

    last = ((1,), (1,))
    first = ((0,), (0,))
    partial = (
        dot(flat(gate_grad_all), gate_weight, last) + dot(flat(up_grad_all), up_weight, last)
    ).astype(BF)
    input_piece = scatter_sum(partial.reshape(token_all.shape)).astype(BF).reshape(8, rows // 8, width)
    inverse = jnp.zeros((8,), jnp.int32).at[order].set(jnp.arange(8, dtype=jnp.int32))
    input_grad = jnp.concatenate(
        [lax.dynamic_index_in_dim(input_piece, inverse[i], 0, keepdims=False) for i in range(8)]
    )
    gate_weight_grad = dot(flat(token_all), flat(gate_grad_all), first).astype(BF)
    up_weight_grad = dot(flat(token_all), flat(up_grad_all), first).astype(BF)
    down_weight_grad = dot(flat(hidden_all), flat(grad_all), first).astype(BF)
    return (input_grad, gate_weight_grad, up_weight_grad, down_weight_grad)


def solution(mesh):
    placed = (P("col", "row"), P("col", "row"), P("row", "col"), P("row", "col"), P("col", "row"))
    return jax.shard_map(
        on_device,
        mesh=mesh,
        in_specs=placed,
        out_specs=(P("col", "row"), P("row", "col"), P("row", "col"), P("col", "row")),
        check_vma=False,
    )
```

```python
import jax
import jax.numpy as jnp
from jax import lax
from jax.experimental import pallas as pl
from jax.experimental.pallas import tpu as pltpu
from jax.sharding import PartitionSpec as P

AXES = ("row", "col")
NZ, NC, NY, NX = 4, 2, 4, 4
COMING = (0, 3, 2, 1)
BF, F32 = jnp.bfloat16, jnp.float32


def dev(z, c, y, x):
    return ((z % NZ) * NC + c) * (NY * NX) + (y % NY) * NX + x % NX


def grid_pairs(target):
    pairs = []
    for z in range(NZ):
        for c in range(NC):
            for y in range(NY):
                for x in range(NX):
                    pairs.append((dev(z, c, y, x), target(z, c, y, x)))
    return pairs


def along_first(step):
    return grid_pairs(lambda z, c, y, x: dev(z, c, y, x + step) if c == 0 else dev(z, c, y + step, x))


def along_second(step):
    return grid_pairs(lambda z, c, y, x: dev(z, c, y + step, x) if c == 0 else dev(z, c, y, x + step))


def along_z(step):
    return grid_pairs(lambda z, c, y, x: dev(z + step if c == 0 else z - step, c, y, x))


def to_partner():
    return grid_pairs(lambda z, c, y, x: dev(z, 1 - c, y, x))


def permute(value, pairs):
    return lax.ppermute(value, AXES, pairs)


def dot(left, right, dims):
    return lax.dot_general(left, right, (dims, ((), ())), preferred_element_type=F32)


def places(core, z):
    out = []
    for half in range(2):
        owner = (core + half) % 2
        sign = 1 - 2 * owner
        for k in COMING:
            out.append(owner * NZ + (z + sign * k + NZ) % NZ)
    return out


def holders(core, z):
    out = []
    for owner in range(2):
        sign = 1 - 2 * owner
        half = (core + owner) % 2
        for quarter in range(NZ):
            out.append(sign * (z - quarter) % NZ * 2 + half)
    return out


def pick(pieces, order):
    return jnp.stack([lax.dynamic_index_in_dim(pieces, i, 0, keepdims=False) for i in order])


def take(order, *sources):
    count = sources[0].shape[0]

    def body(order_ref, *refs):
        ins, outs, sems = refs[: len(sources)], refs[len(sources) : -1], refs[-1]
        copies = []
        for j, (src, dst) in enumerate(zip(ins, outs)):
            for i in range(count):
                copies.append(pltpu.make_async_copy(src.at[order_ref[i]], dst.at[i], sems.at[j * count + i]))
        for copy in copies:
            copy.start()
        for copy in copies:
            copy.wait()

    return pl.pallas_call(
        body,
        grid_spec=pltpu.PrefetchScalarGridSpec(
            num_scalar_prefetch=1,
            grid=(),
            in_specs=[pl.BlockSpec(memory_space=pl.ANY)] * len(sources),
            out_specs=[pl.BlockSpec(memory_space=pltpu.VMEM)] * len(sources),
            scratch_shapes=[pltpu.SemaphoreType.DMA((len(sources) * count,))],
        ),
        out_shape=[jax.ShapeDtypeStruct(v.shape, v.dtype) for v in sources],
        cost_estimate=pl.CostEstimate(flops=0, bytes_accessed=2 * sum(v.size * 2 for v in sources), transcendentals=0),
    )(jnp.stack(order).astype(jnp.int32), *sources)


def take_plane(blocks, source, inward):
    if inward:
        count, halves, js, rows, width = source.shape
        shape = js, halves, count, rows, width
    else:
        js, halves, count, rows, width = source.shape
        shape = count, js, halves, rows, width

    def body(order_ref, src, dst, sems):
        copies = []
        for i in range(count):
            for h in range(halves):
                for j in range(js):
                    at = (i * halves + h) * js + j
                    if inward:
                        ends = src.at[order_ref[i], h, j], dst.at[j, h, i]
                    else:
                        ends = src.at[j, h, order_ref[i]], dst.at[i, j, h]
                    copies.append(pltpu.make_async_copy(*ends, sems.at[at]))
        for copy in copies:
            copy.start()
        for copy in copies:
            copy.wait()

    return pl.pallas_call(
        body,
        grid_spec=pltpu.PrefetchScalarGridSpec(
            num_scalar_prefetch=1,
            grid=(),
            in_specs=[pl.BlockSpec(memory_space=pl.ANY)],
            out_specs=pl.BlockSpec(memory_space=pltpu.VMEM),
            scratch_shapes=[pltpu.SemaphoreType.DMA((count * halves * js,))],
        ),
        out_shape=jax.ShapeDtypeStruct(shape, source.dtype),
        cost_estimate=pl.CostEstimate(flops=0, bytes_accessed=4 * source.size, transcendentals=0),
    )(jnp.stack(blocks).astype(jnp.int32), source)


def tie(value, *others):
    return lax.optimization_barrier((value, *others))[0]


def ring_direct(value, along):
    far, after, before = (permute(value, along(s)) for s in (2, -1, 1))
    return jnp.stack([value, after, far, before])


def ring_gather(value, along):
    half = value.shape[0] // 2
    after = permute(value, along(-1))
    before = permute(value, along(1))
    low = permute(after[:half], along(-1))
    high = permute(before[half:], along(1))
    return jnp.stack([value, after, jnp.concatenate([low, high]), before])


def ring_sum(slices, along):
    half = slices[0].shape[0] // 2
    low = permute(slices[2][:half], along(1))
    high = permute(slices[2][half:], along(-1))
    up = jnp.concatenate([(slices[1][:half].astype(F32) + low.astype(F32)).astype(BF), slices[1][half:]])
    down = jnp.concatenate([slices[3][:half], (slices[3][half:].astype(F32) + high.astype(F32)).astype(BF)])
    total = slices[0].astype(F32) + permute(up, along(1)).astype(F32) + permute(down, along(-1)).astype(F32)
    return total, (low, high)


def direct_sum(slices, along):
    return sum((permute(slices[i], along(i)).astype(F32) for i in (2, 3, 1)), slices[0].astype(F32))


def scatter_sum(value):
    part, early = ring_sum([value[:, :, s] for s in range(4)], along_second)
    part = part.astype(BF)
    return direct_sum([part[:, :, s] for s in range(4)], along_first), early, part


def term(rows, weight, dims):
    lead = rows.shape[:-1]
    out = dot(rows.reshape(-1, rows.shape[-1]), weight, dims).astype(BF)
    return out.reshape(*lead, out.shape[-1])


def terms(rows, weight, dims):
    theirs = permute(term(rows[:, 1], weight, dims), to_partner())
    mine = term(rows[:, 0], weight, dims)
    return lambda j: mine[j].astype(F32) + jnp.swapaxes(theirs[j], 0, 1).astype(F32)


def reduce_ring(both, came):
    for j in (2, 3):
        came = permute((came.astype(F32) + both(j)).astype(BF), along_z(1))
    return came.astype(F32) + both(0)


def gather_ring(piece):
    mine = [piece]
    for _ in range(3):
        mine.append(permute(mine[-1], along_z(1)))
    return mine


def with_partner(mine):
    return jnp.stack([jnp.stack([m, jnp.swapaxes(permute(m, to_partner()), 0, 1)]) for m in mine])


def flat(value):
    return value.reshape(-1, value.shape[-1])


ROWS, LAST, FIRST = ((1,), (0,)), ((1,), (1,)), ((0,), (0,))


def on_device(tokens, out_grad, gate_weight, up_weight, down_weight):
    row, col = lax.axis_index("row"), lax.axis_index("col")
    z, core = row // NC, row % NC
    y, x = col // NX, col % NX
    rows, width = tokens.shape
    piece = rows // 8
    token_piece, grad_piece = take(
        places(core, z), tokens.reshape(8, piece, width), out_grad.reshape(8, piece, width)
    )
    near = ring_direct(token_piece.reshape(2, NZ, piece, width), along_first)
    grad_plane = lax.all_gather(tie(grad_piece, near), "col", axis=0)
    token_all = ring_gather(near, along_second).transpose(3, 2, 0, 1, 4, 5)
    blocks = []
    for i in range(4):
        for j in range(4):
            dy, dx = jnp.where(core == 0, i, j), jnp.where(core == 0, j, i)
            blocks.append((y + dy) % NY * NX + (x + dx) % NX)

    gate_both = terms(token_all, gate_weight, ROWS)
    up_both = terms(token_all, up_weight, ROWS)
    gate_came, up_came = (permute(both(1).astype(BF), along_z(1)) for both in (gate_both, up_both))
    grad_all = take_plane(blocks, grad_plane.reshape(16, 2, NZ, piece, width), True).reshape(token_all.shape)
    grad_all = tie(grad_all, gate_came, up_came)
    back_both = terms(grad_all, down_weight, LAST)
    gate_sum = reduce_ring(gate_both, gate_came)
    up_sum = reduce_ring(up_both, up_came)
    back_sum = reduce_ring(back_both, permute(back_both(1).astype(BF), along_z(1)))
    sigma = jax.nn.sigmoid(gate_sum)
    hidden = (gate_sum * sigma * up_sum).astype(BF)
    up_grad = (back_sum * gate_sum * sigma).astype(BF)
    gate_grad = (back_sum * up_sum * sigma * (1.0 + gate_sum * (1.0 - sigma))).astype(BF)

    gate_grads, up_grads = gather_ring(gate_grad), gather_ring(up_grad)
    hiddens = gather_ring(tie(hidden, gate_grads[3], up_grads[3]))

    def partial_of(gate_part, up_part):
        both = dot(flat(gate_part), gate_weight, LAST) + dot(flat(up_part), up_weight, LAST)
        return both.astype(BF).reshape(2, 2, 4, 4, piece, width)

    gate_0, up_0 = with_partner(gate_grads[:2]), with_partner(up_grads[:2])
    partial_0 = tie(partial_of(gate_0, up_0), gate_grads[3], up_grads[3])
    sums_0 = dot(flat(token_all[:2]), flat(gate_0), FIRST), dot(flat(token_all[:2]), flat(up_0), FIRST)
    gate_1, up_1 = with_partner(gate_grads[2:]), with_partner(up_grads[2:])
    input_piece, early, late = scatter_sum(jnp.concatenate([partial_0, partial_of(gate_1, up_1)]))
    gate_1 = tie(gate_1, *early)
    up_1 = tie(up_1, late)

    input_piece = input_piece.astype(BF).reshape(8, piece, width)
    input_grad = pick(input_piece, holders(core, z)).reshape(rows, width)
    gate_weight_grad = (sums_0[0] + dot(flat(token_all[2:]), flat(gate_1), FIRST)).astype(BF)
    up_weight_grad = (sums_0[1] + dot(flat(token_all[2:]), flat(up_1), FIRST)).astype(BF)
    down_weight_grad = dot(flat(with_partner(hiddens)), flat(grad_all), FIRST).astype(BF)
    return (input_grad, gate_weight_grad, up_weight_grad, down_weight_grad)


def solution(mesh):
    placed = (P("col", "row"), P("col", "row"), P("row", "col"), P("row", "col"), P("col", "row"))
    return jax.shard_map(
        on_device,
        mesh=mesh,
        in_specs=placed,
        out_specs=(P("col", "row"), P("row", "col"), P("row", "col"), P("col", "row")),
        check_vma=False,
    )
```

```python
import jax
import jax.numpy as jnp
from jax import lax
from jax.experimental import pallas as pl
from jax.experimental.pallas import tpu as pltpu
from jax.sharding import PartitionSpec as P

AXES = ("row", "col")
NZ, NC, NY, NX = 4, 2, 4, 4
COMING = (0, 3, 2, 1)
BF, F32 = jnp.bfloat16, jnp.float32


def dev(z, c, y, x):
    return ((z % NZ) * NC + c) * (NY * NX) + (y % NY) * NX + x % NX


def grid_pairs(target):
    pairs = []
    for z in range(NZ):
        for c in range(NC):
            for y in range(NY):
                for x in range(NX):
                    pairs.append((dev(z, c, y, x), target(z, c, y, x)))
    return pairs


def along_first(step):
    return grid_pairs(lambda z, c, y, x: dev(z, c, y, x + step) if c == 0 else dev(z, c, y + step, x))


def along_second(step):
    return grid_pairs(lambda z, c, y, x: dev(z, c, y + step, x) if c == 0 else dev(z, c, y, x + step))


def along_z(step):
    return grid_pairs(lambda z, c, y, x: dev(z + step if c == 0 else z - step, c, y, x))


def to_partner():
    return grid_pairs(lambda z, c, y, x: dev(z, 1 - c, y, x))


def permute(value, pairs):
    return lax.ppermute(value, AXES, pairs)


def dot(left, right, dims):
    return lax.dot_general(left, right, (dims, ((), ())), preferred_element_type=F32)


def places(core, z):
    out = []
    for half in range(2):
        owner = (core + half) % 2
        sign = 1 - 2 * owner
        for k in COMING:
            out.append(owner * NZ + (z + sign * k + NZ) % NZ)
    return out


def holders(core, z):
    out = []
    for owner in range(2):
        sign = 1 - 2 * owner
        half = (core + owner) % 2
        for quarter in range(NZ):
            out.append(sign * (z - quarter) % NZ * 2 + half)
    return out


def pick(pieces, order):
    return jnp.stack([lax.dynamic_index_in_dim(pieces, i, 0, keepdims=False) for i in order])


def take(order, *sources):
    count = sources[0].shape[0]

    def body(order_ref, *refs):
        ins, outs, sems = refs[: len(sources)], refs[len(sources) : -1], refs[-1]
        copies = []
        for j, (src, dst) in enumerate(zip(ins, outs)):
            for i in range(count):
                copies.append(pltpu.make_async_copy(src.at[order_ref[i]], dst.at[i], sems.at[j * count + i]))
        for copy in copies:
            copy.start()
        for copy in copies:
            copy.wait()

    return pl.pallas_call(
        body,
        grid_spec=pltpu.PrefetchScalarGridSpec(
            num_scalar_prefetch=1,
            grid=(),
            in_specs=[pl.BlockSpec(memory_space=pl.ANY)] * len(sources),
            out_specs=[pl.BlockSpec(memory_space=pltpu.VMEM)] * len(sources),
            scratch_shapes=[pltpu.SemaphoreType.DMA((len(sources) * count,))],
        ),
        out_shape=[jax.ShapeDtypeStruct(v.shape, v.dtype) for v in sources],
        cost_estimate=pl.CostEstimate(flops=0, bytes_accessed=2 * sum(v.size * 2 for v in sources), transcendentals=0),
    )(jnp.stack(order).astype(jnp.int32), *sources)


def tie(value, *others):
    return lax.optimization_barrier((value, *others))[0]


def ring_direct(value, along):
    far, after, before = (permute(value, along(s)) for s in (2, -1, 1))
    return jnp.stack([value, after, far, before])


def ring_gather(value, along):
    half = value.shape[0] // 2
    after = permute(value, along(-1))
    before = permute(value, along(1))
    low = permute(after[:half], along(-1))
    high = permute(before[half:], along(1))
    return jnp.stack([value, after, jnp.concatenate([low, high]), before])


def ring_sum(slices, along):
    half = slices[0].shape[0] // 2
    low = permute(slices[2][:half], along(1))
    high = permute(slices[2][half:], along(-1))
    up = jnp.concatenate([(slices[1][:half].astype(F32) + low.astype(F32)).astype(BF), slices[1][half:]])
    down = jnp.concatenate([slices[3][:half], (slices[3][half:].astype(F32) + high.astype(F32)).astype(BF)])
    total = slices[0].astype(F32) + permute(up, along(1)).astype(F32) + permute(down, along(-1)).astype(F32)
    return total, (low, high)


def direct_sum(slices, along):
    return sum((permute(slices[i], along(i)).astype(F32) for i in (2, 3, 1)), slices[0].astype(F32))


def scatter_sum(slices):
    part, early = ring_sum(slices, along_second)
    part = part.astype(BF)
    return direct_sum([part[:, :, s] for s in range(4)], along_first), early, part


def term(rows, weight, dims):
    lead = rows.shape[:-1]
    out = dot(rows.reshape(-1, rows.shape[-1]), weight, dims).astype(BF)
    return out.reshape(*lead, out.shape[-1])


def terms(rows, weight, dims):
    theirs = permute(term(rows[:, 1], weight, dims), to_partner())
    mine = term(rows[:, 0], weight, dims)
    return lambda j: mine[j].astype(F32) + jnp.swapaxes(theirs[j], 0, 1).astype(F32)


def added(both, came, j):
    return (came.astype(F32) + both(j)).astype(BF)


def gather_ring(piece):
    mine = [piece]
    for _ in range(3):
        mine.append(permute(mine[-1], along_z(1)))
    return mine


def with_partner(mine):
    return jnp.stack([jnp.stack([m, jnp.swapaxes(permute(m, to_partner()), 0, 1)]) for m in mine])


def flat(value):
    return value.reshape(-1, value.shape[-1])


ROWS, LAST, FIRST = ((1,), (0,)), ((1,), (1,)), ((0,), (0,))


def on_device(tokens, out_grad, gate_weight, up_weight, down_weight):
    row, col = lax.axis_index("row"), lax.axis_index("col")
    z, core = row // NC, row % NC
    y, x = col // NX, col % NX
    rows, width = tokens.shape
    piece = rows // 8
    token_piece, grad_piece = take(
        places(core, z), tokens.reshape(8, piece, width), out_grad.reshape(8, piece, width)
    )
    near = ring_direct(token_piece.reshape(2, NZ, piece, width), along_first)
    token_plane = ring_gather(near, along_second)
    grad_near = ring_direct(tie(grad_piece, near).reshape(2, NZ, piece, width), along_first)
    grad_plane = ring_gather(tie(grad_near, token_plane), along_second)
    token_all = token_plane.transpose(3, 2, 0, 1, 4, 5)

    gate_both = terms(token_all, gate_weight, ROWS)
    up_both = terms(token_all, up_weight, ROWS)
    gate_came, up_came = (permute(both(1).astype(BF), along_z(1)) for both in (gate_both, up_both))
    grad_all = grad_plane.transpose(3, 2, 0, 1, 4, 5)
    back_both = terms(grad_all, down_weight, LAST)
    cames = [gate_came, up_came, permute(back_both(1).astype(BF), along_z(1))]
    sums = []
    for both, came in zip((gate_both, up_both, back_both), cames):
        for j in (2, 3):
            came = permute(added(both, came, j), along_z(1))
        sums.append(came.astype(F32) + both(0))
    gate_sum, up_sum, back_sum = sums
    sigma = jax.nn.sigmoid(gate_sum)
    hidden = (gate_sum * sigma * up_sum).astype(BF)
    up_grad = (back_sum * gate_sum * sigma).astype(BF)
    gate_grad = (back_sum * up_sum * sigma * (1.0 + gate_sum * (1.0 - sigma))).astype(BF)

    gate_grads, up_grads = gather_ring(gate_grad), gather_ring(up_grad)
    hiddens = gather_ring(tie(hidden, gate_grads[3], up_grads[3]))

    def partial_of(gate_part, up_part):
        both = dot(flat(gate_part), gate_weight, LAST) + dot(flat(up_part), up_weight, LAST)
        return both.astype(BF).reshape(*gate_part.shape[:-1], width)

    gate_0, up_0 = with_partner(gate_grads[:2]), with_partner(up_grads[:2])
    partial_0 = tie(partial_of(gate_0, up_0), gate_grads[3], up_grads[3])
    sums_0 = dot(flat(token_all[:2]), flat(gate_0), FIRST), dot(flat(token_all[:2]), flat(up_0), FIRST)
    gate_1, up_1 = with_partner(gate_grads[2:]), with_partner(up_grads[2:])
    input_piece, early, late = scatter_sum(
        [jnp.concatenate([partial_0[:, :, s], partial_of(gate_1[:, :, s], up_1[:, :, s])]) for s in range(4)]
    )
    gate_1 = tie(gate_1, *early)
    up_1 = tie(up_1, *early)

    input_piece = input_piece.astype(BF).reshape(8, piece, width)
    input_grad = pick(input_piece, holders(core, z)).reshape(rows, width)
    gate_weight_grad = (sums_0[0] + dot(flat(token_all[2:]), flat(gate_1), FIRST)).astype(BF)
    up_weight_grad = (sums_0[1] + dot(flat(token_all[2:]), flat(up_1), FIRST)).astype(BF)
    down_weight_grad = dot(flat(tie(with_partner(hiddens), late)), flat(grad_all), FIRST).astype(BF)
    return (input_grad, gate_weight_grad, up_weight_grad, down_weight_grad)


def solution(mesh):
    placed = (P("col", "row"), P("col", "row"), P("row", "col"), P("row", "col"), P("col", "row"))
    return jax.shard_map(
        on_device,
        mesh=mesh,
        in_specs=placed,
        out_specs=(P("col", "row"), P("row", "col"), P("row", "col"), P("col", "row")),
        check_vma=False,
    )
```

```python
import jax
import jax.numpy as jnp
from jax import lax
from jax.experimental import pallas as pl
from jax.experimental.layout import Layout, with_layout_constraint
from jax.experimental.pallas import tpu as pltpu
from jax.sharding import PartitionSpec as P

AXES = ("row", "col")
NZ, NC, NY, NX = 4, 2, 4, 4
COMING = (0, 3, 2, 1)
BF, F32 = jnp.bfloat16, jnp.float32


def dev(z, c, y, x):
    return ((z % NZ) * NC + c) * (NY * NX) + (y % NY) * NX + x % NX


def grid_pairs(target):
    pairs = []
    for z in range(NZ):
        for c in range(NC):
            for y in range(NY):
                for x in range(NX):
                    pairs.append((dev(z, c, y, x), target(z, c, y, x)))
    return pairs


def along_first(step):
    return grid_pairs(lambda z, c, y, x: dev(z, c, y, x + step) if c == 0 else dev(z, c, y + step, x))


def along_second(step):
    return grid_pairs(lambda z, c, y, x: dev(z, c, y + step, x) if c == 0 else dev(z, c, y, x + step))


def along_z(step):
    return grid_pairs(lambda z, c, y, x: dev(z + step if c == 0 else z - step, c, y, x))


def to_partner():
    return grid_pairs(lambda z, c, y, x: dev(z, 1 - c, y, x))


def permute(value, pairs):
    return lax.ppermute(value, AXES, pairs)


def dot(left, right, dims):
    return lax.dot_general(left, right, (dims, ((), ())), preferred_element_type=F32)


def places(core, z):
    out = []
    for half in range(2):
        owner = (core + half) % 2
        sign = 1 - 2 * owner
        for k in COMING:
            out.append(owner * NZ + (z + sign * k + NZ) % NZ)
    return out


def holders(core, z):
    out = []
    for owner in range(2):
        sign = 1 - 2 * owner
        half = (core + owner) % 2
        for quarter in range(NZ):
            out.append(sign * (z - quarter) % NZ * 2 + half)
    return out


def pick(pieces, order):
    return jnp.stack([lax.dynamic_index_in_dim(pieces, i, 0, keepdims=False) for i in order])


def take(order, *sources):
    count = sources[0].shape[0]

    def body(order_ref, *refs):
        ins, outs, sems = refs[: len(sources)], refs[len(sources) : -1], refs[-1]
        copies = []
        for j, (src, dst) in enumerate(zip(ins, outs)):
            for i in range(count):
                copies.append(pltpu.make_async_copy(src.at[order_ref[i]], dst.at[i], sems.at[j * count + i]))
        for copy in copies:
            copy.start()
        for copy in copies:
            copy.wait()

    return pl.pallas_call(
        body,
        grid_spec=pltpu.PrefetchScalarGridSpec(
            num_scalar_prefetch=1,
            grid=(),
            in_specs=[pl.BlockSpec(memory_space=pl.ANY)] * len(sources),
            out_specs=[pl.BlockSpec(memory_space=pltpu.VMEM)] * len(sources),
            scratch_shapes=[pltpu.SemaphoreType.DMA((len(sources) * count,))],
        ),
        out_shape=[jax.ShapeDtypeStruct(v.shape, v.dtype) for v in sources],
        cost_estimate=pl.CostEstimate(flops=0, bytes_accessed=2 * sum(v.size * 2 for v in sources), transcendentals=0),
    )(jnp.stack(order).astype(jnp.int32), *sources)


def tie(value, *others):
    return lax.optimization_barrier((value, *others))[0]


def ring_direct(value, along):
    far, after, before = (permute(value, along(s)) for s in (2, -1, 1))
    return jnp.stack([value, after, far, before])


def ring_gather(value, along):
    half = value.shape[0] // 2
    after = permute(value, along(-1))
    before = permute(value, along(1))
    low = permute(after[:half], along(-1))
    high = permute(before[half:], along(1))
    return jnp.stack([value, after, jnp.concatenate([low, high]), before])


def ring_sum(low, high, slices, along):
    half = low.shape[0]
    up = jnp.concatenate([(slices[1][:half].astype(F32) + low.astype(F32)).astype(BF), slices[1][half:]])
    down = jnp.concatenate([slices[3][:half], (slices[3][half:].astype(F32) + high.astype(F32)).astype(BF)])
    return slices[0].astype(F32) + permute(up, along(1)).astype(F32) + permute(down, along(-1)).astype(F32)


def direct_sum(slices, along):
    return sum((permute(slices[i], along(i)).astype(F32) for i in (2, 3, 1)), slices[0].astype(F32))


def term(rows, weight, dims):
    lead = rows.shape[:-1]
    out = dot(rows.reshape(-1, rows.shape[-1]), weight, dims).astype(BF)
    return out.reshape(*lead, out.shape[-1])


def terms(rows, weight, dims):
    theirs = permute(term(rows[:, 1], weight, dims), to_partner())
    mine = term(rows[:, 0], weight, dims)
    return lambda j: mine[j].astype(F32) + jnp.swapaxes(theirs[j], 0, 1).astype(F32)


def added(both, came, j):
    return (came.astype(F32) + both(j)).astype(BF)


def gather_ring(piece):
    mine = [piece]
    for _ in range(3):
        mine.append(permute(mine[-1], along_z(1)))
    return mine


def with_partner(mine):
    return jnp.stack([jnp.stack([m, jnp.swapaxes(permute(m, to_partner()), 0, 1)]) for m in mine])


def flat(value):
    return value.reshape(-1, value.shape[-1])


ROWS, LAST, FIRST = ((1,), (0,)), ((1,), (1,)), ((0,), (0,))


def on_device(tokens, out_grad, gate_weight, up_weight, down_weight):
    row, col = lax.axis_index("row"), lax.axis_index("col")
    z, core = row // NC, row % NC
    y, x = col // NX, col % NX
    rows, width = tokens.shape
    piece = rows // 8
    token_piece, grad_piece = take(
        places(core, z), tokens.reshape(8, piece, width), out_grad.reshape(8, piece, width)
    )
    near = ring_direct(token_piece.reshape(2, NZ, piece, width), along_first)
    token_plane = ring_gather(near, along_second)
    grad_near = ring_direct(tie(grad_piece, near).reshape(2, NZ, piece, width), along_first)
    grad_plane = ring_gather(tie(grad_near, token_plane), along_second)
    token_all = token_plane.transpose(3, 2, 0, 1, 4, 5)

    gate_both = terms(token_all, gate_weight, ROWS)
    up_both = terms(token_all, up_weight, ROWS)
    gate_came, up_came = (permute(both(1).astype(BF), along_z(1)) for both in (gate_both, up_both))
    grad_all = grad_plane.transpose(3, 2, 0, 1, 4, 5)
    back_both = terms(grad_all, down_weight, LAST)
    cames = [gate_came, up_came, permute(back_both(1).astype(BF), along_z(1))]
    sums = []
    for both, came in zip((gate_both, up_both, back_both), cames):
        for j in (2, 3):
            came = permute(added(both, came, j), along_z(1))
        sums.append(came.astype(F32) + both(0))
    gate_sum, up_sum, back_sum = sums
    sigma = jax.nn.sigmoid(gate_sum)
    hidden = (gate_sum * sigma * up_sum).astype(BF)
    up_grad = (back_sum * gate_sum * sigma).astype(BF)
    gate_grad = (back_sum * up_sum * sigma * (1.0 + gate_sum * (1.0 - sigma))).astype(BF)

    gate_grad, up_grad, hidden = (
        with_layout_constraint(value, Layout((0, 1, 2, 3))) for value in (gate_grad, up_grad, hidden)
    )
    gate_grads, up_grads = gather_ring(gate_grad), gather_ring(up_grad)
    hiddens = gather_ring(tie(hidden, gate_grads[3], up_grads[3]))

    def partial_of(gate_part, up_part):
        both = dot(flat(gate_part), gate_weight, LAST) + dot(flat(up_part), up_weight, LAST)
        return both.astype(BF).reshape(*gate_part.shape[:-1], width)

    gate_0, up_0 = with_partner(gate_grads[:2]), with_partner(up_grads[:2])
    partial_0 = tie(partial_of(gate_0, up_0), gate_grads[3], up_grads[3])
    gate_1, up_1 = with_partner(gate_grads[2:]), with_partner(up_grads[2:])
    low = permute(partial_0[:, :, 2], along_second(1))
    high = permute(partial_of(gate_1[:, :, 2], up_1[:, :, 2]), along_second(-1))
    gate_0, up_0, gate_2, up_2, _ = lax.optimization_barrier((gate_0, up_0, gate_1, up_1, low))
    sums_0 = dot(flat(token_all[:2]), flat(gate_0), FIRST), dot(flat(token_all[:2]), flat(up_0), FIRST)
    slices = [
        None if s == 2 else jnp.concatenate([partial_0[:, :, s], partial_of(gate_2[:, :, s], up_2[:, :, s])])
        for s in range(4)
    ]
    late = ring_sum(low, high, slices, along_second).astype(BF)
    input_piece = direct_sum([late[:, :, s] for s in range(4)], along_first)
    gate_1, up_1 = lax.optimization_barrier((gate_1, up_1, high))[:2]

    input_piece = input_piece.astype(BF).reshape(8, piece, width)
    input_grad = pick(input_piece, holders(core, z)).reshape(rows, width)
    gate_weight_grad = (sums_0[0] + dot(flat(token_all[2:]), flat(gate_1), FIRST)).astype(BF)
    up_weight_grad = (sums_0[1] + dot(flat(token_all[2:]), flat(up_1), FIRST)).astype(BF)
    down_weight_grad = dot(flat(tie(with_partner(hiddens), late)), flat(grad_all), FIRST).astype(BF)
    return (input_grad, gate_weight_grad, up_weight_grad, down_weight_grad)


def solution(mesh):
    placed = (P("col", "row"), P("col", "row"), P("row", "col"), P("row", "col"), P("col", "row"))
    return jax.shard_map(
        on_device,
        mesh=mesh,
        in_specs=placed,
        out_specs=(P("col", "row"), P("row", "col"), P("row", "col"), P("col", "row")),
        check_vma=False,
    )
```

```python
import jax
import jax.numpy as jnp
from jax import lax
from jax.experimental import pallas as pl
from jax.experimental.layout import Layout, with_layout_constraint
from jax.experimental.pallas import tpu as pltpu
from jax.sharding import PartitionSpec as P

AXES = ("row", "col")
NZ, NC, NY, NX = 4, 2, 4, 4
COMING = (0, 3, 2, 1)
BF, F32 = jnp.bfloat16, jnp.float32


def dev(z, c, y, x):
    return ((z % NZ) * NC + c) * (NY * NX) + (y % NY) * NX + x % NX


def grid_pairs(target):
    pairs = []
    for z in range(NZ):
        for c in range(NC):
            for y in range(NY):
                for x in range(NX):
                    pairs.append((dev(z, c, y, x), target(z, c, y, x)))
    return pairs


def along_first(step):
    return grid_pairs(lambda z, c, y, x: dev(z, c, y, x + step) if c == 0 else dev(z, c, y + step, x))


def along_second(step):
    return grid_pairs(lambda z, c, y, x: dev(z, c, y + step, x) if c == 0 else dev(z, c, y, x + step))


def along_z(step):
    return grid_pairs(lambda z, c, y, x: dev(z + step if c == 0 else z - step, c, y, x))


def to_partner():
    return grid_pairs(lambda z, c, y, x: dev(z, 1 - c, y, x))


def permute(value, pairs):
    return lax.ppermute(value, AXES, pairs)


def dot(left, right, dims):
    return lax.dot_general(left, right, (dims, ((), ())), preferred_element_type=F32)


def places(core, z):
    out = []
    for half in range(2):
        owner = (core + half) % 2
        sign = 1 - 2 * owner
        for k in COMING:
            out.append(owner * NZ + (z + sign * k + NZ) % NZ)
    return out


def holders(core, z):
    out = []
    for owner in range(2):
        sign = 1 - 2 * owner
        half = (core + owner) % 2
        for quarter in range(NZ):
            out.append(sign * (z - quarter) % NZ * 2 + half)
    return out


def pick(pieces, order):
    return jnp.stack([lax.dynamic_index_in_dim(pieces, i, 0, keepdims=False) for i in order])


def take(order, *sources):
    count = sources[0].shape[0]

    def body(order_ref, *refs):
        ins, outs, sems = refs[: len(sources)], refs[len(sources) : -1], refs[-1]
        copies = []
        for j, (src, dst) in enumerate(zip(ins, outs)):
            for i in range(count):
                copies.append(pltpu.make_async_copy(src.at[order_ref[i]], dst.at[i], sems.at[j * count + i]))
        for copy in copies:
            copy.start()
        for copy in copies:
            copy.wait()

    return pl.pallas_call(
        body,
        grid_spec=pltpu.PrefetchScalarGridSpec(
            num_scalar_prefetch=1,
            grid=(),
            in_specs=[pl.BlockSpec(memory_space=pl.ANY)] * len(sources),
            out_specs=[pl.BlockSpec(memory_space=pltpu.VMEM)] * len(sources),
            scratch_shapes=[pltpu.SemaphoreType.DMA((len(sources) * count,))],
        ),
        out_shape=[jax.ShapeDtypeStruct(v.shape, v.dtype) for v in sources],
        cost_estimate=pl.CostEstimate(flops=0, bytes_accessed=2 * sum(v.size * 2 for v in sources), transcendentals=0),
    )(jnp.stack(order).astype(jnp.int32), *sources)


def tie(value, *others):
    return lax.optimization_barrier((value, *others))[0]


def ring_direct(value, along):
    far, after, before = (permute(value, along(s)) for s in (2, -1, 1))
    return jnp.stack([value, after, far, before])


def ring_gather(value, along):
    half = value.shape[0] // 2
    after = permute(value, along(-1))
    before = permute(value, along(1))
    low = permute(after[:half], along(-1))
    high = permute(before[half:], along(1))
    return jnp.stack([value, after, jnp.concatenate([low, high]), before])


def ring_sum(low, high, slices, along):
    half = low.shape[0]
    up = jnp.concatenate([(slices[1][:half].astype(F32) + low.astype(F32)).astype(BF), slices[1][half:]])
    down = jnp.concatenate([slices[3][:half], (slices[3][half:].astype(F32) + high.astype(F32)).astype(BF)])
    return slices[0].astype(F32) + permute(up, along(1)).astype(F32) + permute(down, along(-1)).astype(F32)


def direct_sum(slices, along):
    return sum((permute(slices[i], along(i)).astype(F32) for i in (2, 3, 1)), slices[0].astype(F32))


def term(rows, weight, dims):
    lead = rows.shape[:-1]
    out = dot(rows.reshape(-1, rows.shape[-1]), weight, dims).astype(BF)
    return out.reshape(*lead, out.shape[-1])


def terms(rows, weight, dims):
    theirs = permute(term(rows[:, 1], weight, dims), to_partner())
    mine = term(rows[:, 0], weight, dims)
    return lambda j: mine[j].astype(F32) + jnp.swapaxes(theirs[j], 0, 1).astype(F32)


def added(both, came, j):
    return (came.astype(F32) + both(j)).astype(BF)


def gather_ring(piece):
    mine = [piece]
    for _ in range(3):
        mine.append(permute(mine[-1], along_z(1)))
    return mine


def with_partner(mine):
    return jnp.stack([jnp.stack([m, jnp.swapaxes(permute(m, to_partner()), 0, 1)]) for m in mine])


def flat(value):
    return value.reshape(-1, value.shape[-1])


ROWS, LAST, FIRST = ((1,), (0,)), ((1,), (1,)), ((0,), (0,))


def on_device(tokens, out_grad, gate_weight, up_weight, down_weight):
    row, col = lax.axis_index("row"), lax.axis_index("col")
    z, core = row // NC, row % NC
    y, x = col // NX, col % NX
    rows, width = tokens.shape
    piece = rows // 8
    token_piece, grad_piece = take(
        places(core, z), tokens.reshape(8, piece, width), out_grad.reshape(8, piece, width)
    )
    near = ring_direct(jnp.stack([token_piece, grad_piece]).reshape(2, 2, NZ, piece, width), along_first)
    token_plane = ring_gather(near[:, 0], along_second)
    grad_plane = ring_gather(near[:, 1], along_second)
    token_all = token_plane.transpose(3, 2, 0, 1, 4, 5)

    gate_both = terms(token_all, gate_weight, ROWS)
    up_both = terms(token_all, up_weight, ROWS)
    gate_came, up_came = (permute(both(1).astype(BF), along_z(1)) for both in (gate_both, up_both))
    grad_all = grad_plane.transpose(3, 2, 0, 1, 4, 5)
    back_both = terms(grad_all, down_weight, LAST)
    cames = [gate_came, up_came, permute(back_both(1).astype(BF), along_z(1))]
    sums = []
    for both, came in zip((gate_both, up_both, back_both), cames):
        for j in (2, 3):
            came = permute(added(both, came, j), along_z(1))
        sums.append(came.astype(F32) + both(0))
    gate_sum, up_sum, back_sum = sums
    sigma = jax.nn.sigmoid(gate_sum)
    hidden = (gate_sum * sigma * up_sum).astype(BF)
    up_grad = (back_sum * gate_sum * sigma).astype(BF)
    gate_grad = (back_sum * up_sum * sigma * (1.0 + gate_sum * (1.0 - sigma))).astype(BF)

    gate_grad, up_grad, hidden = (
        with_layout_constraint(value, Layout((0, 1, 2, 3))) for value in (gate_grad, up_grad, hidden)
    )
    gate_grads, up_grads = gather_ring(gate_grad), gather_ring(up_grad)
    hiddens = gather_ring(tie(hidden, gate_grads[3], up_grads[3]))

    def partial_of(gate_part, up_part):
        both = dot(flat(gate_part), gate_weight, LAST) + dot(flat(up_part), up_weight, LAST)
        return both.astype(BF).reshape(*gate_part.shape[:-1], width)

    gate_0, up_0 = with_partner(gate_grads[:2]), with_partner(up_grads[:2])
    partial_0 = tie(partial_of(gate_0, up_0), gate_grads[3], up_grads[3])
    gate_1, up_1 = with_partner(gate_grads[2:]), with_partner(up_grads[2:])
    low = permute(partial_0[:, :, 2], along_second(1))
    high = permute(partial_of(gate_1[:, :, 2], up_1[:, :, 2]), along_second(-1))
    gate_0, up_0, gate_2, up_2, _ = lax.optimization_barrier((gate_0, up_0, gate_1, up_1, low))
    sums_0 = dot(flat(token_all[:2]), flat(gate_0), FIRST), dot(flat(token_all[:2]), flat(up_0), FIRST)
    slices = [
        None if s == 2 else jnp.concatenate([partial_0[:, :, s], partial_of(gate_2[:, :, s], up_2[:, :, s])])
        for s in range(4)
    ]
    late = ring_sum(low, high, slices, along_second).astype(BF)
    input_piece = direct_sum([late[:, :, s] for s in range(4)], along_first)
    gate_1, up_1 = lax.optimization_barrier((gate_1, up_1, high))[:2]

    input_piece = input_piece.astype(BF).reshape(8, piece, width)
    input_grad = pick(input_piece, holders(core, z)).reshape(rows, width)
    gate_weight_grad = (sums_0[0] + dot(flat(token_all[2:]), flat(gate_1), FIRST)).astype(BF)
    up_weight_grad = (sums_0[1] + dot(flat(token_all[2:]), flat(up_1), FIRST)).astype(BF)
    down_weight_grad = dot(flat(tie(with_partner(hiddens), late)), flat(grad_all), FIRST).astype(BF)
    return (input_grad, gate_weight_grad, up_weight_grad, down_weight_grad)


def solution(mesh):
    placed = (P("col", "row"), P("col", "row"), P("row", "col"), P("row", "col"), P("col", "row"))
    return jax.shard_map(
        on_device,
        mesh=mesh,
        in_specs=placed,
        out_specs=(P("col", "row"), P("row", "col"), P("row", "col"), P("col", "row")),
        check_vma=False,
    )
```

```python
import jax
import jax.numpy as jnp
from jax import lax
from jax.experimental import pallas as pl
from jax.experimental.layout import Layout, with_layout_constraint
from jax.experimental.pallas import tpu as pltpu
from jax.sharding import PartitionSpec as P

AXES = ("row", "col")
NZ, NC, NY, NX = 4, 2, 4, 4
COMING = (0, 3, 2, 1)
BF, F32 = jnp.bfloat16, jnp.float32


def dev(z, c, y, x):
    return ((z % NZ) * NC + c) * (NY * NX) + (y % NY) * NX + x % NX


def grid_pairs(target):
    pairs = []
    for z in range(NZ):
        for c in range(NC):
            for y in range(NY):
                for x in range(NX):
                    pairs.append((dev(z, c, y, x), target(z, c, y, x)))
    return pairs


def along_first(step):
    return grid_pairs(lambda z, c, y, x: dev(z, c, y, x + step) if c == 0 else dev(z, c, y + step, x))


def along_second(step):
    return grid_pairs(lambda z, c, y, x: dev(z, c, y + step, x) if c == 0 else dev(z, c, y, x + step))


def along_z(step):
    return grid_pairs(lambda z, c, y, x: dev(z + step if c == 0 else z - step, c, y, x))


def to_partner():
    return grid_pairs(lambda z, c, y, x: dev(z, 1 - c, y, x))


def permute(value, pairs):
    return lax.ppermute(value, AXES, pairs)


def dot(left, right, dims):
    return lax.dot_general(left, right, (dims, ((), ())), preferred_element_type=F32)


def places(core, z):
    out = []
    for half in range(2):
        owner = (core + half) % 2
        sign = 1 - 2 * owner
        for k in COMING:
            out.append(owner * NZ + (z + sign * k + NZ) % NZ)
    return out


def holders(core, z):
    out = []
    for owner in range(2):
        sign = 1 - 2 * owner
        half = (core + owner) % 2
        for quarter in range(NZ):
            out.append(sign * (z - quarter) % NZ * 2 + half)
    return out


def pick(pieces, order):
    return jnp.stack([lax.dynamic_index_in_dim(pieces, i, 0, keepdims=False) for i in order])


def take(order, *sources):
    count = sources[0].shape[0]

    def body(order_ref, *refs):
        ins, outs, sems = refs[: len(sources)], refs[len(sources) : -1], refs[-1]
        copies = []
        for j, (src, dst) in enumerate(zip(ins, outs)):
            for i in range(count):
                copies.append(pltpu.make_async_copy(src.at[order_ref[i]], dst.at[i], sems.at[j * count + i]))
        for copy in copies:
            copy.start()
        for copy in copies:
            copy.wait()

    return pl.pallas_call(
        body,
        grid_spec=pltpu.PrefetchScalarGridSpec(
            num_scalar_prefetch=1,
            grid=(),
            in_specs=[pl.BlockSpec(memory_space=pl.ANY)] * len(sources),
            out_specs=[pl.BlockSpec(memory_space=pltpu.VMEM)] * len(sources),
            scratch_shapes=[pltpu.SemaphoreType.DMA((len(sources) * count,))],
        ),
        out_shape=[jax.ShapeDtypeStruct(v.shape, v.dtype) for v in sources],
        cost_estimate=pl.CostEstimate(flops=0, bytes_accessed=2 * sum(v.size * 2 for v in sources), transcendentals=0),
    )(jnp.stack(order).astype(jnp.int32), *sources)


def tie(value, *others):
    return lax.optimization_barrier((value, *others))[0]


def ring_direct(value, along):
    far, after, before = (permute(value, along(s)) for s in (2, -1, 1))
    return jnp.stack([value, after, far, before])


def ring_gather(value, along):
    half = value.shape[0] // 2
    after = permute(value, along(-1))
    before = permute(value, along(1))
    low = permute(after[:half], along(-1))
    high = permute(before[half:], along(1))
    return jnp.stack([value, after, jnp.concatenate([low, high]), before])


def ring_sum(low, high, slices, along):
    half = low.shape[0]
    up = jnp.concatenate([(slices[1][:half].astype(F32) + low.astype(F32)).astype(BF), slices[1][half:]])
    down = jnp.concatenate([slices[3][:half], (slices[3][half:].astype(F32) + high.astype(F32)).astype(BF)])
    return slices[0].astype(F32) + permute(up, along(1)).astype(F32) + permute(down, along(-1)).astype(F32)


def direct_sum(slices, along):
    return sum((permute(slices[i], along(i)).astype(F32) for i in (2, 3, 1)), slices[0].astype(F32))


def term(rows, weight, dims):
    lead = rows.shape[:-1]
    out = dot(rows.reshape(-1, rows.shape[-1]), weight, dims).astype(BF)
    return out.reshape(*lead, out.shape[-1])


def terms(rows, weight, dims):
    theirs = permute(term(rows[:, 1], weight, dims), to_partner())
    mine = term(rows[:, 0], weight, dims)
    return lambda j: mine[j].astype(F32) + jnp.swapaxes(theirs[j], 0, 1).astype(F32)


def added(both, came, j):
    return (came.astype(F32) + both(j)).astype(BF)


def gather_ring(piece):
    mine = [piece]
    for _ in range(3):
        mine.append(permute(mine[-1], along_z(1)))
    return mine


def with_partner(mine):
    return jnp.stack([jnp.stack([m, jnp.swapaxes(permute(m, to_partner()), 0, 1)]) for m in mine])


def flat(value):
    return value.reshape(-1, value.shape[-1])


ROWS, LAST, FIRST = ((1,), (0,)), ((1,), (1,)), ((0,), (0,))


def on_device(tokens, out_grad, gate_weight, up_weight, down_weight):
    row, col = lax.axis_index("row"), lax.axis_index("col")
    z, core = row // NC, row % NC
    y, x = col // NX, col % NX
    rows, width = tokens.shape
    piece = rows // 8
    token_piece, grad_piece = take(
        places(core, z), tokens.reshape(8, piece, width), out_grad.reshape(8, piece, width)
    )
    near = ring_direct(jnp.stack([token_piece, grad_piece]).reshape(2, 2, NZ, piece, width), along_first)
    token_plane = ring_gather(near[:, 0], along_second)
    grad_plane = ring_gather(near[:, 1], along_second)
    token_all = token_plane.transpose(3, 2, 0, 1, 4, 5)

    gate_both = terms(token_all, gate_weight, ROWS)
    up_both = terms(token_all, up_weight, ROWS)
    gate_came, up_came = (permute(both(1).astype(BF), along_z(1)) for both in (gate_both, up_both))
    grad_all = grad_plane.transpose(3, 2, 0, 1, 4, 5)
    back_both = terms(grad_all, down_weight, LAST)
    cames = [gate_came, up_came, permute(back_both(1).astype(BF), along_z(1))]
    sums = []
    for both, came in zip((gate_both, up_both, back_both), cames):
        for j in (2, 3):
            came = permute(added(both, came, j), along_z(1))
        sums.append(came.astype(F32) + both(0))
    gate_sum, up_sum, back_sum = sums
    sigma = jax.nn.sigmoid(gate_sum)
    hidden = (gate_sum * sigma * up_sum).astype(BF)
    up_grad = (back_sum * gate_sum * sigma).astype(BF)
    gate_grad = (back_sum * up_sum * sigma * (1.0 + gate_sum * (1.0 - sigma))).astype(BF)

    gate_grad, up_grad, hidden = (
        with_layout_constraint(value, Layout((0, 1, 2, 3))) for value in (gate_grad, up_grad, hidden)
    )
    gate_grads, up_grads = gather_ring(gate_grad), gather_ring(up_grad)
    hiddens = gather_ring(tie(hidden, gate_grads[3], up_grads[3]))

    def partial_of(gate_part, up_part):
        both = dot(flat(gate_part), gate_weight, LAST) + dot(flat(up_part), up_weight, LAST)
        return both.astype(BF).reshape(*gate_part.shape[:-1], width)

    gate_0, up_0 = with_partner(gate_grads[:2]), with_partner(up_grads[:2])
    partial_0 = tie(partial_of(gate_0, up_0), gate_grads[3], up_grads[3])
    gate_1, up_1 = with_partner(gate_grads[2:]), with_partner(up_grads[2:])
    low = permute(partial_0[:, :, 2], along_second(1))
    high = permute(partial_of(gate_1[:, :, 2], up_1[:, :, 2]), along_second(-1))
    gate_2, up_2, _ = lax.optimization_barrier((gate_1, up_1, low))
    gate_0, up_0, _ = lax.optimization_barrier((gate_0, up_0, high))
    sums_0 = dot(flat(token_all[:2]), flat(gate_0), FIRST), dot(flat(token_all[:2]), flat(up_0), FIRST)
    slices = [
        None if s == 2 else jnp.concatenate([partial_0[:, :, s], partial_of(gate_2[:, :, s], up_2[:, :, s])])
        for s in range(4)
    ]
    late = ring_sum(low, high, slices, along_second).astype(BF)
    input_piece = direct_sum([late[:, :, s] for s in range(4)], along_first)
    gate_1, up_1 = lax.optimization_barrier((gate_1, up_1, high))[:2]

    input_piece = input_piece.astype(BF).reshape(8, piece, width)
    input_grad = pick(input_piece, holders(core, z)).reshape(rows, width)
    gate_weight_grad = (sums_0[0] + dot(flat(token_all[2:]), flat(gate_1), FIRST)).astype(BF)
    up_weight_grad = (sums_0[1] + dot(flat(token_all[2:]), flat(up_1), FIRST)).astype(BF)
    down_weight_grad = dot(flat(tie(with_partner(hiddens), late)), flat(grad_all), FIRST).astype(BF)
    return (input_grad, gate_weight_grad, up_weight_grad, down_weight_grad)


def solution(mesh):
    placed = (P("col", "row"), P("col", "row"), P("row", "col"), P("row", "col"), P("col", "row"))
    return jax.shard_map(
        on_device,
        mesh=mesh,
        in_specs=placed,
        out_specs=(P("col", "row"), P("row", "col"), P("row", "col"), P("col", "row")),
        check_vma=False,
    )
```
